32 devices in a mesh: groups: 2 (over x), expert: 16 (over z, y, core).
Axes of the slice: x: 2, y: 2, z: 4, core: 2. Of those that a mesh axis runs over, the one named last changes fastest.
Arguments:
- tokens: bfloat16 [4096, 3584], P(('groups', 'expert')), parts along dimension 0, may hold values from -6 to 6
- expert_ids: int32 [4096, 8], P(('groups', 'expert')), parts along dimension 0, may hold values from 0 to 255, all different within a row
- lengths: int32 [2], P('groups'), parts along dimension 0, may hold values from 1024 to 2048
- router: bfloat16 [256, 3584], P('expert'), may hold values from -0.09375 to 0.09375
- w_gate: bfloat16 [16, 3584, 512], P('expert'), may hold values from -0.09375 to 0.09375
- w_up: bfloat16 [16, 3584, 512], P('expert'), may hold values from -0.09375 to 0.09375
- w_down: bfloat16 [16, 512, 3584], P('expert'), may hold values from -0.125 to 0.125
Outputs:
- mixed: bfloat16 [4096, 3584], P(('groups', 'expert')), parts along dimension 0
The draws below stay inside these ranges and needn't reach their ends.
There are 2 independent parts, one for each index of `groups`. The reference program is written for one: setup_inputs(seed, part) draws one part's arguments, and reference() takes and returns one part's arrays. A program takes and returns all parts, laid end to end along the dimension named above; an argument that names none is the same for every part. Nothing has to cross between parts.
Inputs may be any that keep to these rules, and one draw needn't show every extreme that they name: `expert_ids`: each row names 8 different experts.
All inputs are finite; a program needn't handle non-finite values.
Results may differ from the reference program's by a relative error of at most 0.0057.
Values may be sent and summed in bfloat16 or wider, within the bound.
A program may use at most 64 MiB of HBM per device.

```python
import jax
import jax.numpy as jnp
from jax import lax

D = 3584
FF = 2048
EXPERTS = 256
TOP = 8
SPLIT = 4
SEQ_LEN = 2048
TOK_DEV = 128
FF_DEV = 512
CAP = 4
TOKENS = 2048
SEQS = 1
N_EXPERT = 16


def steps_of(own_key, dims, split, smallest, top_value):
    factor_of, own = 1.0, jax.random.fold_in(own_key, 6)
    for axis_at, shards_of in split:
        heights = jnp.exp(jax.random.uniform(jax.random.fold_in(own, axis_at), (shards_of,), jnp.float32, smallest / len(split), top_value / len(split)))
        factor_of = factor_of * jnp.repeat(heights, dims[axis_at] // shards_of).reshape([-1 if axis == axis_at else 1 for axis in range(len(dims))])
    return factor_of


def distinct(stream_key, rows, count, top, lift):
    order = jax.random.permutation(jax.random.fold_in(stream_key, 1), count)
    favour = order
    for power in range(3):
        favour = favour * favour // count
    favour = favour * lift // count
    chance = jax.random.randint(jax.random.fold_in(stream_key, 2), (rows, count), 0, 4096) + favour
    sure = jax.random.permutation(jax.random.fold_in(stream_key, 3), rows)[jnp.arange(count) % rows]
    chance = jnp.where(jnp.arange(rows)[:, None] == sure[None, :], 1 << 14, chance)
    score = chance * count + jnp.arange(count)
    return lax.top_k(score.astype(jnp.int32), top)[1].astype(jnp.int32)


def normal_values(key, dims, scale, most, shards=(), kind=jnp.bfloat16):
    values = scale * jax.random.normal(key, dims, jnp.float32)
    if shards:
        values = values * steps_of(key, dims, shards, -0.22, 0.18)
    return jnp.clip(values, -most, most).astype(kind)


def setup_inputs(seed: int = 0, part: int = 0) -> dict:
    streams_of = jax.random.split(jax.random.key(seed), 8)
    part_splits = jax.random.split(jax.random.fold_in(streams_of[7], part), 8)
    return {
        "tokens": normal_values(part_splits[0], (TOKENS, D), 1.0, 6.0, ((0, 16),)),
        "expert_ids": distinct(part_splits[1], TOKENS, EXPERTS, TOP, 512),
        "lengths": jax.random.randint(part_splits[2], (SEQS,), SEQ_LEN // 2, SEQ_LEN + 1).astype(jnp.int32),
        "router": normal_values(streams_of[3], (EXPERTS, D), D ** -0.5, 0.09375, ((0, 16),)),
        "w_gate": normal_values(streams_of[4], (N_EXPERT, D, FF_DEV), D ** -0.5, 0.09375, ((0, 16),)),
        "w_up": normal_values(streams_of[5], (N_EXPERT, D, FF_DEV), D ** -0.5, 0.09375, ((0, 16),)),
        "w_down": normal_values(streams_of[6], (N_EXPERT, FF_DEV, D), FF ** -0.5, 0.125, ((0, 16),)),
    }


def reference(tokens, expert_ids, lengths, router, w_gate, w_up, w_down):
    n_dev = N_EXPERT
    window = N_EXPERT // SPLIT
    scores = jax.nn.sigmoid(jnp.dot(tokens, router.T, preferred_element_type=jnp.float32))
    picked = jnp.take_along_axis(scores, expert_ids, axis=1)
    route_gate = 2.5 * picked / jnp.sum(picked, axis=1, keepdims=True)
    position = jnp.arange(TOKENS, dtype=jnp.int32)
    is_live = (position % SEQ_LEN) < lengths[position // SEQ_LEN]
    flat_ids = expert_ids.reshape(n_dev, TOK_DEV * TOP)
    live_routes = jnp.repeat(is_live, TOP).reshape(n_dev, TOK_DEV * TOP)
    in_window = ((flat_ids[:, :, None] == jnp.arange(window, dtype=jnp.int32)[None, None, :]) & live_routes[:, :, None]).astype(jnp.int32)
    slot_index = (jnp.cumsum(in_window, axis=1) - in_window).astype(jnp.int32)
    kept_route = in_window * (slot_index < CAP).astype(jnp.int32)
    slot_onehot = kept_route[..., None] * (slot_index[..., None] == jnp.arange(CAP, dtype=jnp.int32)).astype(jnp.int32)
    slot_onehot = slot_onehot.reshape(n_dev, TOK_DEV, TOP, window, CAP).astype(jnp.float32)
    dispatch = jnp.sum(slot_onehot, axis=2)
    combine = jnp.einsum("btkwc,btk->bwct", slot_onehot, route_gate.reshape(n_dev, TOK_DEV, TOP), precision=lax.Precision.HIGHEST)
    blocks = tokens.reshape(n_dev, TOK_DEV, D).astype(jnp.float32)
    rows = jnp.einsum("btwc,btd->wbcd", dispatch, blocks, precision=lax.Precision.HIGHEST).astype(jnp.bfloat16)
    gate_slices = w_gate.reshape(window, SPLIT, D, FF_DEV)
    up_slices = w_up.reshape(window, SPLIT, D, FF_DEV)
    down_slices = w_down.reshape(window, SPLIT, FF_DEV, D)

    def one_expert(which):
        flat_rows = rows[which].reshape(n_dev * CAP, D)
        total = jnp.zeros((n_dev * CAP, D), jnp.float32)
        for part_index in range(SPLIT):
            gate_act = jnp.dot(flat_rows, gate_slices[which, part_index], preferred_element_type=jnp.float32)
            up_act = jnp.dot(flat_rows, up_slices[which, part_index], preferred_element_type=jnp.float32)
            hidden = (jax.nn.silu(gate_act) * up_act).astype(jnp.bfloat16)
            partial_value = jnp.dot(hidden, down_slices[which, part_index], preferred_element_type=jnp.float32).astype(jnp.bfloat16)
            total = total + partial_value.astype(jnp.float32)
        return total.reshape(n_dev, CAP, D)

    expert_out = lax.map(one_expert, jnp.arange(window, dtype=jnp.int32))
    mixed = jnp.einsum("bwct,wbcd->btd", combine, expert_out, precision=lax.Precision.HIGHEST)
    return mixed.reshape(TOKENS, D).astype(jnp.bfloat16)
```

```python
import functools

import jax
import jax.numpy as jnp
from jax import lax
from jax.experimental import pallas as pl
from jax.experimental.pallas import tpu as pltpu
from jax.sharding import PartitionSpec as P

SPLIT = 4
SEQ_LEN = 2048
CAP = 4
FOLD = 16 // CAP
F32, BF16 = jnp.float32, jnp.bfloat16


def mod(a, b):
    return lax.rem(a, jnp.int32(b))


def iota(shape, axis):
    return lax.broadcasted_iota(jnp.int32, shape, axis)


def dot(a, b):
    return jnp.dot(a, b, preferred_element_type=F32)


def dot_nt(a, b):
    return lax.dot_general(a, b, (((1,), (1,)), ((), ())), preferred_element_type=F32)


def kernel(
    n, local, tokens_hbm, ids_hbm, len_hbm, router_hbm, gate_hbm, up_hbm, down_hbm, out_hbm,
    tok, ids, length, wg, wu, wd, routed, fold_out, fold_in, x, hidden, part, reduced, back_out, back,
    logit, logits, mask, num_mask, onehot, out,
    load_sem, out_sem, disp_s, disp_r, rout_s, rout_r, fwd_s, fwd_r, red_s, red_r, back_s, back_r, log_s, log_r,
):
    win = n // SPLIT
    rows = win * 16
    per = win * CAP
    rows_tok, width = tok.shape
    quarter = width // FOLD
    lanes = logit.shape[1]
    epad = routed.shape[1]
    me = lax.axis_index("expert")
    w = lax.div(me, jnp.int32(SPLIT))
    r = me - w * SPLIT

    def other(dw, dr):
        return {"expert": mod(w + (dw + win), win) * SPLIT + mod(r + (dr + SPLIT), SPLIT)}

    loads = [
        pltpu.make_async_copy(src, dst, load_sem.at[i])
        for i, (src, dst) in enumerate(
            [
                (ids_hbm, ids), (len_hbm, length), (tokens_hbm, tok), (router_hbm, routed.at[0]),
                (gate_hbm.at[0], wg), (up_hbm.at[0], wu), (down_hbm.at[0], wd),
            ]
        )
    ]
    for load in loads:
        load.start()

    barrier = pltpu.get_barrier_semaphore()
    for step in range(1, n):
        pl.semaphore_signal(
            barrier, inc=1, device_id={"expert": mod(me + step, n)}, device_id_type=pl.DeviceIdType.MESH
        )

    def send(src, dst, s_sem, r_sem, device):
        copy = pltpu.make_async_remote_copy(
            src_ref=src, dst_ref=dst, send_sem=s_sem, recv_sem=r_sem,
            device_id=device, device_id_type=pl.DeviceIdType.MESH,
        )
        return copy

    loads[0].wait()
    loads[1].wait()
    ids_b = ids[...].astype(F32).astype(BF16)
    eye = (iota((8, 8), 0) == iota((8, 8), 1)).astype(F32).astype(BF16)
    ids_t = dot_nt(eye, ids_b).astype(jnp.int32)
    first = me * rows_tok
    alive = mod(first, SEQ_LEN) + iota((rows, rows_tok), 1) < length[lax.div(first, jnp.int32(SEQ_LEN))]
    row = iota((rows, rows_tok), 0)
    expert = mod(w + lax.div(row, jnp.int32(16)), win)
    chosen = ids_t[0:1, :] == expert
    for k in range(1, ids_t.shape[0]):
        chosen = chosen | (ids_t[k : k + 1, :] == expert)
    inside = jnp.where(chosen & alive, 1.0, 0.0)
    earlier = (iota((rows_tok, rows_tok), 0) < iota((rows_tok, rows_tok), 1)).astype(F32).astype(BF16)
    before = dot(inside.astype(BF16), earlier)
    hot = jnp.where(before == mod(row, CAP).astype(F32), inside, 0.0)
    onehot[...] = hot
    turn = mod(lax.div(row, jnp.int32(CAP)), FOLD)

    loads[2].wait()
    folded = jnp.zeros((rows, quarter), F32)
    for q in range(FOLD):
        picked = jnp.where(turn == q, hot, 0.0).astype(BF16)
        folded = folded + dot(picked, tok[:, q * quarter : (q + 1) * quarter])
    folded = folded.astype(BF16)
    fold_in[0, 0] = folded[:16]
    for dw in range(1, win):
        fold_out[dw] = folded[dw * 16 : (dw + 1) * 16]

    pl.semaphore_wait(barrier, n - 1)
    sends = []
    disp = [None]
    for dw in range(1, win):
        disp.append(send(fold_out.at[dw], fold_in.at[0, dw], disp_s.at[dw], disp_r.at[dw], other(dw, 0)))
        disp[dw].start()
    fwd = {}
    for dr in range(1, SPLIT):
        fwd[0, dr] = send(
            fold_in.at[0, 0], fold_in.at[dr, 0], fwd_s.at[0, dr], fwd_r.at[0, dr], other(0, dr)
        )
        fwd[0, dr].start()
    loads[3].wait()
    rout = [None]
    for dw in range(1, win):
        rout.append(send(routed.at[0], routed.at[dw], rout_s.at[dw], rout_r.at[dw], other(dw, 0)))
        rout[dw].start()

    for dw in range(1, win):
        disp[dw].wait_recv()
        for dr in range(1, SPLIT):
            fwd[dw, dr] = send(
                fold_in.at[0, dw], fold_in.at[dr, dw], fwd_s.at[dw, dr], fwd_r.at[dw, dr], other(0, dr)
            )
            fwd[dw, dr].start()

    slot_ids = dot(hot.astype(BF16), ids_b)
    srow = iota((rows, lanes), 0)
    lane = iota((rows, lanes), 1)
    slot_dw = lax.div(srow, jnp.int32(16))
    lane_dw = lax.div(lane, jnp.int32(epad))
    lane_e = lane - lane_dw * epad
    good = (lane_dw < win) & (lane_e < local)
    mine = mod(w + slot_dw, win)
    for i in range(SPLIT):
        chunk = mod(w + slot_dw - lane_dw + 2 * win, win) * SPLIT + mod(r + i, SPLIT)
        which = jnp.where(good, chunk * local + lane_e, -1)
        as_float = which.astype(F32)
        hit = jnp.zeros((rows, lanes), F32)
        for k in range(ids_b.shape[1]):
            hit = jnp.where(as_float == slot_ids[:, k : k + 1], 1.0, hit)
        mask[i] = hit
        num_mask[i] = jnp.where(which == mine, 1.0, 0.0)

    prow, pcol = iota((rows, rows), 0), iota((rows, rows), 1)
    q_of, dw_of, c_of = lax.div(prow, jnp.int32(per)), lax.div(mod(prow, per), jnp.int32(CAP)), mod(prow, CAP)
    perm = (pcol == dw_of * 16 + q_of * CAP + c_of).astype(F32).astype(BF16)
    for i in range(SPLIT):
        if i:
            for dw in range(win):
                fwd[dw, i].wait_recv()
        plain = dot(perm, fold_in[i].reshape(rows, quarter)).astype(BF16)
        for q in range(FOLD):
            x[i * per : (i + 1) * per, q * quarter : (q + 1) * quarter] = plain[q * per : (q + 1) * per]

    loads[4].wait()
    loads[5].wait()
    units = wg.shape[1]
    half = units // 2
    for piece in range(2):
        cols = slice(piece * half, (piece + 1) * half)
        g = dot(x[...], wg[:, cols])
        u = dot(x[...], wu[:, cols])
        hidden[:, cols] = (g * jax.nn.sigmoid(g) * u).astype(BF16)
    loads[6].wait()
    red = {}
    for q in range(FOLD):
        part[q] = dot(hidden[...], wd[:, q * quarter : (q + 1) * quarter]).astype(BF16).reshape(
            SPLIT, per, quarter
        )
        for i in range(1, SPLIT):
            red[q, i] = send(
                part.at[q, i], reduced.at[q, i], red_s.at[q, i], red_r.at[q, i], other(0, -i)
            )
            red[q, i].start()

    for dw in range(1, win):
        rout[dw].wait_recv()
    logit[...] = jnp.zeros_like(logit)
    logit[:, : win * epad] = dot_nt(x[...], routed[...].reshape(win * epad, width))
    logs = {}
    for i in range(SPLIT):
        for dw in range(win):
            src = logit.at[pl.ds(i * per + dw // 2 * 8, 8)]
            if i or dw:
                logs[i, dw] = send(src, logits.at[i, dw], log_s.at[i, dw], log_r.at[i, dw], other(-dw, -i))
                logs[i, dw].start()
            else:
                logits[0, 0] = logit[:8]

    frow, fcol = iota((rows, per), 0), iota((rows, per), 1)
    place = lax.div(frow, jnp.int32(16)) * CAP + mod(frow, CAP)
    total = jnp.zeros((rows, quarter), F32)
    for q in range(FOLD):
        summed = part[q, 0].astype(F32)
        for i in range(1, SPLIT):
            red[q, i].wait_recv()
            summed = summed + reduced[q, i].astype(F32)
        spread = ((fcol == place) & (mod(lax.div(frow, jnp.int32(CAP)), FOLD) == q)).astype(F32).astype(BF16)
        total = total + dot(spread, summed.astype(BF16))
    total = total.astype(BF16)
    back[0] = total[:16]
    backs = [None]
    for dw in range(1, win):
        back_out[dw] = total[dw * 16 : (dw + 1) * 16]
        backs.append(send(back_out.at[dw], back.at[dw], back_s.at[dw], back_r.at[dw], other(-dw, 0)))
        backs[dw].start()

    for pair in logs:
        logs[pair].wait_recv()
    erow, ecol = iota((rows, win * 8), 0), iota((rows, win * 8), 1)
    edw = lax.div(erow, jnp.int32(16))
    expand = jnp.where(ecol == edw * 8 + mod(edw, 2) * CAP + mod(erow, CAP), 1.0, 0.0)
    den = jnp.zeros((rows, 1), F32)
    num = jnp.zeros((rows, 1), F32)
    for i in range(SPLIT):
        spread = jnp.dot(
            expand, logits[i].reshape(win * 8, lanes), preferred_element_type=F32, precision=lax.Precision.HIGHEST
        )
        score = jax.nn.sigmoid(spread)
        den = den + jnp.sum(jnp.where(mask[i] > 0.5, score, 0.0), axis=1, keepdims=True)
        num = num + jnp.sum(jnp.where(num_mask[i] > 0.5, score, 0.0), axis=1, keepdims=True)
    hot = onehot[...]
    filled = jnp.sum(hot, axis=1, keepdims=True) > 0.5
    weight = jnp.where(filled, 2.5 * num / jnp.where(filled, den, 1.0), 0.0)
    combine = (hot * weight).T
    high = combine.astype(BF16).astype(F32)
    middle = (combine - high).astype(BF16).astype(F32)
    low = combine - high - middle
    ccol = mod(lax.div(iota((rows_tok, rows), 1), jnp.int32(CAP)), FOLD)

    for dw in range(1, win):
        backs[dw].wait_recv()
    returned = back[...].reshape(rows, quarter)
    stores = []
    for q in range(FOLD):
        cols = slice(q * quarter, (q + 1) * quarter)
        acc = jnp.zeros((rows_tok, quarter), F32)
        for piece in (high, middle, low):
            acc = acc + dot(jnp.where(ccol == q, piece, 0.0).astype(BF16), returned)
        out[:, cols] = acc.astype(BF16)
        stores.append(pltpu.make_async_copy(out.at[:, cols], out_hbm.at[:, cols], out_sem.at[q]))
        stores[q].start()

    for copies in (disp[1:], rout[1:], backs[1:], fwd.values(), red.values(), logs.values()):
        for copy in copies:
            copy.wait_send()
    for store in stores:
        store.wait()


def shards(tokens, expert_ids, lengths, router, w_gate, w_up, w_down):
    n = lax.axis_size("expert")
    win = n // SPLIT
    rows_tok, width = tokens.shape
    quarter = width // FOLD
    units = w_gate.shape[2]
    local = router.shape[0]
    epad = -(-local // 16) * 16
    if epad != local:
        router = jnp.pad(router, ((0, epad - local), (0, 0)))
    lanes = -(-win * epad // 128) * 128
    rows, per = win * 16, win * CAP
    vmem = pltpu.VMEM
    sems = pltpu.SemaphoreType.DMA
    scratch = [
        vmem((rows_tok, width), BF16),
        vmem(expert_ids.shape, jnp.int32),
        pltpu.SMEM(lengths.shape, jnp.int32),
        vmem((width, units), BF16),
        vmem((width, units), BF16),
        vmem((units, width), BF16),
        vmem((win, epad, width), BF16),
        vmem((win, 16, quarter), BF16),
        vmem((SPLIT, win, 16, quarter), BF16),
        vmem((SPLIT * per, width), BF16),
        vmem((SPLIT * per, units), BF16),
        vmem((FOLD, SPLIT, per, quarter), BF16),
        vmem((FOLD, SPLIT, per, quarter), BF16),
        vmem((win, 16, quarter), BF16),
        vmem((win, 16, quarter), BF16),
        vmem((SPLIT * per, lanes), F32),
        vmem((SPLIT, win, 8, lanes), F32),
        vmem((SPLIT, rows, lanes), F32),
        vmem((SPLIT, rows, lanes), F32),
        vmem((rows, rows_tok), F32),
        vmem((rows_tok, width), BF16),
        sems((7,)),
        sems((FOLD,)),
        *[sems((win,))] * 4,
        *[sems((win, SPLIT))] * 2,
        *[sems((FOLD, SPLIT))] * 2,
        *[sems((win,))] * 2,
        *[sems((SPLIT, win))] * 2,
    ]
    return pl.pallas_call(
        functools.partial(kernel, n, local),
        out_shape=jax.ShapeDtypeStruct((rows_tok, width), BF16),
        in_specs=[pl.BlockSpec(memory_space=pl.ANY)] * 7,
        out_specs=pl.BlockSpec(memory_space=pl.ANY),
        scratch_shapes=scratch,
        compiler_params=pltpu.CompilerParams(
            collective_id=0, has_side_effects=True, vmem_limit_bytes=48 * 1024 * 1024
        ),
    )(tokens, expert_ids, lengths, router, w_gate, w_up, w_down)


def solution(mesh):
    placed = (
        P(("groups", "expert"), None),
        P(("groups", "expert"), None),
        P("groups"),
        P("expert", None),
        P("expert", None, None),
        P("expert", None, None),
        P("expert", None, None),
    )
    return jax.shard_map(
        shards, mesh=mesh, in_specs=placed, out_specs=P(("groups", "expert"), None), check_vma=False
    )
```

```python
import functools

import jax
import jax.numpy as jnp
from jax import lax
from jax.experimental import pallas as pl
from jax.experimental.pallas import tpu as pltpu
from jax.sharding import PartitionSpec as P

SPLIT = 4
SEQ_LEN = 2048
CAP = 4
FOLD = 16 // CAP
F32, BF16 = jnp.float32, jnp.bfloat16


def mod(a, b):
    return lax.rem(a, jnp.int32(b))


def iota(shape, axis):
    return lax.broadcasted_iota(jnp.int32, shape, axis)


def dot(a, b):
    return jnp.dot(a, b, preferred_element_type=F32)


def dot_nt(a, b):
    return lax.dot_general(a, b, (((1,), (1,)), ((), ())), preferred_element_type=F32)


def kernel(
    n, local, tokens_hbm, ids_hbm, len_hbm, router_hbm, gate_hbm, up_hbm, down_hbm, out,
    tok, ids, length, wg, wu, wd, routed, fold_out, fold_in, x, hidden, part, reduced, back_out, back,
    logit, logits, mask, num_mask, onehot,
    load_sem, disp_s, disp_r, rout_s, rout_r, fwd_s, fwd_r, red_s, red_r, back_s, back_r, log_s, log_r,
):
    win = n // SPLIT
    rows = win * 16
    per = win * CAP
    rows_tok, width = tok.shape
    quarter = width // FOLD
    lanes = logit.shape[1]
    epad = routed.shape[1]
    me = lax.axis_index("expert")
    w = lax.div(me, jnp.int32(SPLIT))
    r = me - w * SPLIT

    def other(dw, dr):
        return {"expert": mod(w + (dw + win), win) * SPLIT + mod(r + (dr + SPLIT), SPLIT)}

    loads = [
        pltpu.make_async_copy(src, dst, load_sem.at[i])
        for i, (src, dst) in enumerate(
            [
                (ids_hbm, ids), (len_hbm, length), (tokens_hbm, tok), (router_hbm, routed.at[0]),
                (gate_hbm.at[0], wg), (up_hbm.at[0], wu), (down_hbm.at[0], wd),
            ]
        )
    ]
    for load in loads:
        load.start()

    barrier = pltpu.get_barrier_semaphore()
    for step in range(1, n):
        pl.semaphore_signal(
            barrier, inc=1, device_id={"expert": mod(me + step, n)}, device_id_type=pl.DeviceIdType.MESH
        )

    def send(src, dst, s_sem, r_sem, device):
        copy = pltpu.make_async_remote_copy(
            src_ref=src, dst_ref=dst, send_sem=s_sem, recv_sem=r_sem,
            device_id=device, device_id_type=pl.DeviceIdType.MESH,
        )
        return copy

    loads[0].wait()
    loads[1].wait()
    ids_t = ids[...]
    ids_b = ids_t.astype(F32).astype(BF16)
    first = me * rows_tok
    alive = mod(first, SEQ_LEN) + iota((rows, rows_tok), 1) < length[lax.div(first, jnp.int32(SEQ_LEN))]
    row = iota((rows, rows_tok), 0)
    expert = mod(w + lax.div(row, jnp.int32(16)), win)
    chosen = ids_t[0:1, :] == expert
    for k in range(1, ids_t.shape[0]):
        chosen = chosen | (ids_t[k : k + 1, :] == expert)
    inside = jnp.where(chosen & alive, 1.0, 0.0)
    earlier = (iota((rows_tok, rows_tok), 0) < iota((rows_tok, rows_tok), 1)).astype(F32).astype(BF16)
    before = dot(inside.astype(BF16), earlier)
    hot = jnp.where(before == mod(row, CAP).astype(F32), inside, 0.0)
    onehot[...] = hot
    turn = mod(lax.div(row, jnp.int32(CAP)), FOLD)

    loads[2].wait()
    folded = jnp.zeros((rows, quarter), F32)
    for q in range(FOLD):
        picked = jnp.where(turn == q, hot, 0.0).astype(BF16)
        folded = folded + dot(picked, tok[:, q * quarter : (q + 1) * quarter])
    folded = folded.astype(BF16)
    fold_in[0, 0] = folded[:16]
    for dw in range(1, win):
        fold_out[dw] = folded[dw * 16 : (dw + 1) * 16]

    pl.semaphore_wait(barrier, n - 1)
    sends = []
    disp = [None]
    for dw in range(1, win):
        disp.append(send(fold_out.at[dw], fold_in.at[0, dw], disp_s.at[dw], disp_r.at[dw], other(dw, 0)))
        disp[dw].start()
    fwd = {}
    for dr in range(1, SPLIT):
        fwd[0, dr] = send(
            fold_in.at[0, 0], fold_in.at[dr, 0], fwd_s.at[0, dr], fwd_r.at[0, dr], other(0, dr)
        )
        fwd[0, dr].start()
    loads[3].wait()
    rout = [None]
    for dw in range(1, win):
        rout.append(send(routed.at[0], routed.at[dw], rout_s.at[dw], rout_r.at[dw], other(dw, 0)))
        rout[dw].start()

    for dw in range(1, win):
        disp[dw].wait_recv()
        for dr in range(1, SPLIT):
            fwd[dw, dr] = send(
                fold_in.at[0, dw], fold_in.at[dr, dw], fwd_s.at[dw, dr], fwd_r.at[dw, dr], other(0, dr)
            )
            fwd[dw, dr].start()

    slot_ids = dot_nt(hot.astype(BF16), ids_b)
    srow = iota((rows, lanes), 0)
    lane = iota((rows, lanes), 1)
    slot_dw = lax.div(srow, jnp.int32(16))
    lane_dw = lax.div(lane, jnp.int32(epad))
    lane_e = lane - lane_dw * epad
    good = (lane_dw < win) & (lane_e < local)
    mine = mod(w + slot_dw, win)
    for i in range(SPLIT):
        chunk = mod(w + slot_dw - lane_dw + 2 * win, win) * SPLIT + mod(r + i, SPLIT)
        which = jnp.where(good, chunk * local + lane_e, -1)
        as_float = which.astype(F32)
        hit = jnp.zeros((rows, lanes), F32)
        for k in range(ids_b.shape[0]):
            hit = jnp.where(as_float == slot_ids[:, k : k + 1], 1.0, hit)
        mask[i] = hit
        num_mask[i] = jnp.where(which == mine, 1.0, 0.0)

    prow, pcol = iota((rows, rows), 0), iota((rows, rows), 1)
    q_of, dw_of, c_of = lax.div(prow, jnp.int32(per)), lax.div(mod(prow, per), jnp.int32(CAP)), mod(prow, CAP)
    perm = (pcol == dw_of * 16 + q_of * CAP + c_of).astype(F32).astype(BF16)
    for i in range(SPLIT):
        if i:
            for dw in range(win):
                fwd[dw, i].wait_recv()
        plain = dot(perm, fold_in[i].reshape(rows, quarter)).astype(BF16)
        for q in range(FOLD):
            x[i * per : (i + 1) * per, q * quarter : (q + 1) * quarter] = plain[q * per : (q + 1) * per]

    loads[4].wait()
    loads[5].wait()
    units = wg.shape[1]
    half = units // 2
    for piece in range(2):
        cols = slice(piece * half, (piece + 1) * half)
        g = dot(x[...], wg[:, cols])
        u = dot(x[...], wu[:, cols])
        hidden[:, cols] = (g * jax.nn.sigmoid(g) * u).astype(BF16)
    loads[6].wait()
    red = {}
    for q in range(FOLD):
        part[q] = dot(hidden[...], wd[:, q * quarter : (q + 1) * quarter]).astype(BF16).reshape(
            SPLIT, per, quarter
        )
        for i in range(1, SPLIT):
            red[q, i] = send(
                part.at[q, i], reduced.at[q, i], red_s.at[q, i], red_r.at[q, i], other(0, -i)
            )
            red[q, i].start()

    for dw in range(1, win):
        rout[dw].wait_recv()
    logit[...] = jnp.zeros_like(logit)
    logit[:, : win * epad] = dot_nt(x[...], routed[...].reshape(win * epad, width))
    logs = {}
    for i in range(SPLIT):
        for dw in range(win):
            src = logit.at[pl.ds(i * per + dw // 2 * 8, 8)]
            if i or dw:
                logs[i, dw] = send(src, logits.at[i, dw], log_s.at[i, dw], log_r.at[i, dw], other(-dw, -i))
                logs[i, dw].start()
            else:
                logits[0, 0] = logit[:8]

    frow, fcol = iota((rows, per), 0), iota((rows, per), 1)
    place = lax.div(frow, jnp.int32(16)) * CAP + mod(frow, CAP)
    total = jnp.zeros((rows, quarter), F32)
    for q in range(FOLD):
        summed = part[q, 0].astype(F32)
        for i in range(1, SPLIT):
            red[q, i].wait_recv()
            summed = summed + reduced[q, i].astype(F32)
        spread = ((fcol == place) & (mod(lax.div(frow, jnp.int32(CAP)), FOLD) == q)).astype(F32).astype(BF16)
        total = total + dot(spread, summed.astype(BF16))
    total = total.astype(BF16)
    back[0] = total[:16]
    backs = [None]
    for dw in range(1, win):
        back_out[dw] = total[dw * 16 : (dw + 1) * 16]
        backs.append(send(back_out.at[dw], back.at[dw], back_s.at[dw], back_r.at[dw], other(-dw, 0)))
        backs[dw].start()

    for pair in logs:
        logs[pair].wait_recv()
    erow, ecol = iota((rows, win * 8), 0), iota((rows, win * 8), 1)
    edw = lax.div(erow, jnp.int32(16))
    expand = jnp.where(ecol == edw * 8 + mod(edw, 2) * CAP + mod(erow, CAP), 1.0, 0.0)
    den = jnp.zeros((rows, 1), F32)
    num = jnp.zeros((rows, 1), F32)
    for i in range(SPLIT):
        spread = jnp.dot(
            expand, logits[i].reshape(win * 8, lanes), preferred_element_type=F32, precision=lax.Precision.HIGHEST
        )
        score = jax.nn.sigmoid(spread)
        den = den + jnp.sum(jnp.where(mask[i] > 0.5, score, 0.0), axis=1, keepdims=True)
        num = num + jnp.sum(jnp.where(num_mask[i] > 0.5, score, 0.0), axis=1, keepdims=True)
    hot = onehot[...]
    filled = jnp.sum(hot, axis=1, keepdims=True) > 0.5
    weight = jnp.where(filled, 2.5 * num / jnp.where(filled, den, 1.0), 0.0)
    combine = (hot * weight).T
    high = combine.astype(BF16).astype(F32)
    middle = (combine - high).astype(BF16).astype(F32)
    low = combine - high - middle
    ccol = mod(lax.div(iota((rows_tok, rows), 1), jnp.int32(CAP)), FOLD)

    for dw in range(1, win):
        backs[dw].wait_recv()
    returned = back[...].reshape(rows, quarter)
    for q in range(FOLD):
        cols = slice(q * quarter, (q + 1) * quarter)
        acc = jnp.zeros((rows_tok, quarter), F32)
        for piece in (high, middle, low):
            acc = acc + dot(jnp.where(ccol == q, piece, 0.0).astype(BF16), returned)
        out[:, cols] = acc.astype(BF16)

    for copies in (disp[1:], rout[1:], backs[1:], fwd.values(), red.values(), logs.values()):
        for copy in copies:
            copy.wait_send()


def shards(tokens, expert_ids, lengths, router, w_gate, w_up, w_down):
    n = lax.axis_size("expert")
    win = n // SPLIT
    rows_tok, width = tokens.shape
    quarter = width // FOLD
    units = w_gate.shape[2]
    local = router.shape[0]
    epad = -(-local // 16) * 16
    if epad != local:
        router = jnp.pad(router, ((0, epad - local), (0, 0)))
    lanes = -(-win * epad // 128) * 128
    rows, per = win * 16, win * CAP
    vmem = pltpu.VMEM
    sems = pltpu.SemaphoreType.DMA
    scratch = [
        vmem((rows_tok, width), BF16),
        vmem(expert_ids.shape[::-1], jnp.int32),
        pltpu.SMEM(lengths.shape, jnp.int32),
        vmem((width, units), BF16),
        vmem((width, units), BF16),
        vmem((units, width), BF16),
        vmem((win, epad, width), BF16),
        vmem((win, 16, quarter), BF16),
        vmem((SPLIT, win, 16, quarter), BF16),
        vmem((SPLIT * per, width), BF16),
        vmem((SPLIT * per, units), BF16),
        vmem((FOLD, SPLIT, per, quarter), BF16),
        vmem((FOLD, SPLIT, per, quarter), BF16),
        vmem((win, 16, quarter), BF16),
        vmem((win, 16, quarter), BF16),
        vmem((SPLIT * per, lanes), F32),
        vmem((SPLIT, win, 8, lanes), F32),
        vmem((SPLIT, rows, lanes), F32),
        vmem((SPLIT, rows, lanes), F32),
        vmem((rows, rows_tok), F32),
        sems((7,)),
        *[sems((win,))] * 4,
        *[sems((win, SPLIT))] * 2,
        *[sems((FOLD, SPLIT))] * 2,
        *[sems((win,))] * 2,
        *[sems((SPLIT, win))] * 2,
    ]
    return pl.pallas_call(
        functools.partial(kernel, n, local),
        out_shape=jax.ShapeDtypeStruct((rows_tok, width), BF16),
        in_specs=[pl.BlockSpec(memory_space=pltpu.HBM)] * 7,
        out_specs=pl.BlockSpec(memory_space=pltpu.VMEM),
        scratch_shapes=scratch,
        compiler_params=pltpu.CompilerParams(
            collective_id=0, has_side_effects=True, vmem_limit_bytes=56 * 1024 * 1024
        ),
    )(tokens, expert_ids.T, lengths, router, w_gate, w_up, w_down)


def solution(mesh):
    placed = (
        P(("groups", "expert"), None),
        P(("groups", "expert"), None),
        P("groups"),
        P("expert", None),
        P("expert", None, None),
        P("expert", None, None),
        P("expert", None, None),
    )
    return jax.shard_map(
        shards, mesh=mesh, in_specs=placed, out_specs=P(("groups", "expert"), None), check_vma=False
    )
```

```python
import functools

import jax
import jax.numpy as jnp
from jax import lax
from jax.experimental import pallas as pl
from jax.experimental.pallas import tpu as pltpu
from jax.sharding import PartitionSpec as P

SPLIT = 4
SEQ_LEN = 2048
CAP = 4
FOLD = 16 // CAP
F32, BF16 = jnp.float32, jnp.bfloat16


def mod(a, b):
    return lax.rem(a, jnp.int32(b))


def iota(shape, axis):
    return lax.broadcasted_iota(jnp.int32, shape, axis)


def dot(a, b):
    return jnp.dot(a, b, preferred_element_type=F32)


def dot_nt(a, b):
    return lax.dot_general(a, b, (((1,), (1,)), ((), ())), preferred_element_type=F32)


def kernel(
    n, local, tokens_hbm, ids_hbm, len_hbm, router_hbm, gate_hbm, up_hbm, down_hbm, out,
    tok, ids, length, wg, wu, wd, routed, fold_out, fold_in, x, hidden, part, reduced, back_out, back,
    logit, logits, mask, num_mask, onehot,
    load_sem, disp_s, disp_r, rout_s, rout_r, fwd_s, fwd_r, red_s, red_r, back_s, back_r, log_s, log_r,
):
    win = n // SPLIT
    rows = win * 16
    per = win * CAP
    rows_tok, width = tok.shape
    quarter = width // FOLD
    lanes = logit.shape[1]
    epad = routed.shape[1]
    me = lax.axis_index("expert")
    w = lax.div(me, jnp.int32(SPLIT))
    r = me - w * SPLIT

    def flip(at, bit):
        return at + bit - 2 * bit * mod(lax.div(at, jnp.int32(bit)), 2)

    def place_of(i):
        at = r
        for bit in (1, 2):
            at = flip(at, bit) if i & bit else at
        return at

    def other(dw, i):
        return {"expert": mod(w + (dw + win), win) * SPLIT + place_of(i)}

    loads = [
        pltpu.make_async_copy(src, dst, load_sem.at[i])
        for i, (src, dst) in enumerate(
            [
                (ids_hbm, ids), (len_hbm, length), (tokens_hbm, tok), (router_hbm, routed.at[0]),
                (gate_hbm.at[0], wg), (up_hbm.at[0], wu), (down_hbm.at[0], wd),
            ]
        )
    ]
    for load in loads:
        load.start()

    barrier = pltpu.get_barrier_semaphore()
    for step in range(1, n):
        pl.semaphore_signal(
            barrier, inc=1, device_id={"expert": mod(me + step, n)}, device_id_type=pl.DeviceIdType.MESH
        )

    def send(src, dst, s_sem, r_sem, device):
        copy = pltpu.make_async_remote_copy(
            src_ref=src, dst_ref=dst, send_sem=s_sem, recv_sem=r_sem,
            device_id=device, device_id_type=pl.DeviceIdType.MESH,
        )
        return copy

    loads[0].wait()
    loads[1].wait()
    ids_t = ids[...]
    ids_b = ids_t.astype(F32).astype(BF16)
    first = me * rows_tok
    alive = mod(first, SEQ_LEN) + iota((rows, rows_tok), 1) < length[lax.div(first, jnp.int32(SEQ_LEN))]
    row = iota((rows, rows_tok), 0)
    expert = mod(w + lax.div(row, jnp.int32(16)), win)
    chosen = ids_t[0:1, :] == expert
    for k in range(1, ids_t.shape[0]):
        chosen = chosen | (ids_t[k : k + 1, :] == expert)
    inside = jnp.where(chosen & alive, 1.0, 0.0)
    earlier = (iota((rows_tok, rows_tok), 0) < iota((rows_tok, rows_tok), 1)).astype(F32).astype(BF16)
    before = dot(inside.astype(BF16), earlier)
    hot = jnp.where(before == mod(row, CAP).astype(F32), inside, 0.0)
    onehot[...] = hot
    turn = mod(lax.div(row, jnp.int32(CAP)), FOLD)

    loads[2].wait()
    folded = jnp.zeros((rows, quarter), F32)
    for q in range(FOLD):
        picked = jnp.where(turn == q, hot, 0.0).astype(BF16)
        folded = folded + dot(picked, tok[:, q * quarter : (q + 1) * quarter])
    folded = folded.astype(BF16)
    fold_in[0, 0] = folded[:16]
    for dw in range(1, win):
        fold_out[dw] = folded[dw * 16 : (dw + 1) * 16]

    pl.semaphore_wait(barrier, n - 1)
    sends = []
    disp = [None]
    for dw in range(1, win):
        disp.append(send(fold_out.at[dw], fold_in.at[0, dw], disp_s.at[dw], disp_r.at[dw], other(dw, 0)))
        disp[dw].start()
    fwd = {}

    def forward(src, dst, dw, i):
        fwd[dw, dst] = send(
            fold_in.at[src, dw], fold_in.at[dst, dw], fwd_s.at[dw, dst], fwd_r.at[dw, dst], other(0, i)
        )
        fwd[dw, dst].start()

    for dw in range(win):
        if dw:
            disp[dw].wait_recv()
        forward(0, 2, dw, 2)
        forward(0, 1, dw, 1)

    loads[3].wait()
    rout, arrived = {}, set()

    def push(held):
        bit = (held & -held or win) // 2
        while bit:
            rout[held + bit] = send(
                routed.at[held], routed.at[held + bit], rout_s.at[held + bit], rout_r.at[held + bit],
                {"expert": flip(w, bit) * SPLIT + r},
            )
            rout[held + bit].start()
            bit //= 2

    def low_bit(d):
        return d & -d

    push(0)

    slot_ids = dot_nt(hot.astype(BF16), ids_b)
    srow = iota((rows, lanes), 0)
    lane = iota((rows, lanes), 1)
    slot_dw = lax.div(srow, jnp.int32(16))
    lane_dw = lax.div(lane, jnp.int32(epad))
    lane_e = lane - lane_dw * epad
    good = (lane_dw < win) & (lane_e < local)
    mine = mod(w + slot_dw, win)
    for i in range(SPLIT):
        chunk = (mine ^ lane_dw) * SPLIT + place_of(i)
        which = jnp.where(good, chunk * local + lane_e, -1)
        as_float = which.astype(F32)
        hit = jnp.zeros((rows, lanes), F32)
        for k in range(ids_b.shape[0]):
            hit = jnp.where(as_float == slot_ids[:, k : k + 1], 1.0, hit)
        mask[i] = hit
        num_mask[i] = jnp.where(which == mine, 1.0, 0.0)

    prow, pcol = iota((rows, rows), 0), iota((rows, rows), 1)
    q_of, dw_of, c_of = lax.div(prow, jnp.int32(per)), lax.div(mod(prow, per), jnp.int32(CAP)), mod(prow, CAP)
    perm = (pcol == dw_of * 16 + q_of * CAP + c_of).astype(F32).astype(BF16)
    for dw in range(win):
        fwd[dw, 2].wait_recv()
        forward(2, 3, dw, 1)
    for i in range(SPLIT):
        if i in (1, 3):
            for dw in range(win):
                fwd[dw, i].wait_recv()
        plain = dot(perm, fold_in[i].reshape(rows, quarter)).astype(BF16)
        for q in range(FOLD):
            x[i * per : (i + 1) * per, q * quarter : (q + 1) * quarter] = plain[q * per : (q + 1) * per]

    loads[4].wait()
    loads[5].wait()
    units = wg.shape[1]
    half = units // 2
    for piece in range(2):
        cols = slice(piece * half, (piece + 1) * half)
        g = dot(x[...], wg[:, cols])
        u = dot(x[...], wu[:, cols])
        hidden[:, cols] = (g * jax.nn.sigmoid(g) * u).astype(BF16)
    for held in sorted(range(1, win), key=lambda d: (-low_bit(d), d)):
        if low_bit(held) > 1:
            rout[held].wait_recv()
            arrived.add(held)
            push(held)
    loads[6].wait()
    red = {}

    def give(q, src, dst, i):
        red[q, dst] = send(part.at[q, src], reduced.at[q, dst], red_s.at[q, dst], red_r.at[q, dst], other(0, i))
        red[q, dst].start()

    for q in range(FOLD):
        part[q] = dot(hidden[...], wd[:, q * quarter : (q + 1) * quarter]).astype(BF16).reshape(
            SPLIT, per, quarter
        )
        give(q, 3, 3, 1)
        give(q, 1, 1, 1)
    for q in range(FOLD):
        red[q, 3].wait_recv()
        part[q, 2] = (part[q, 2].astype(F32) + reduced[q, 3].astype(F32)).astype(BF16)
        give(q, 2, 2, 2)

    for held in range(1, win):
        if held not in arrived:
            rout[held].wait_recv()
    logit[...] = jnp.zeros_like(logit)
    logit[:, : win * epad] = dot_nt(x[...], routed[...].reshape(win * epad, width))
    logs = {}
    for i in range(SPLIT):
        for dw in range(win):
            src = logit.at[pl.ds(i * per + dw // 2 * 8, 8)]
            if i or dw:
                logs[i, dw] = send(src, logits.at[i, dw], log_s.at[i, dw], log_r.at[i, dw], other(-dw, i))
                logs[i, dw].start()
            else:
                logits[0, 0] = logit[:8]

    frow, fcol = iota((rows, per), 0), iota((rows, per), 1)
    place = lax.div(frow, jnp.int32(16)) * CAP + mod(frow, CAP)
    total = jnp.zeros((rows, quarter), F32)
    for q in range(FOLD):
        summed = part[q, 0].astype(F32)
        for i in (1, 2):
            red[q, i].wait_recv()
            summed = summed + reduced[q, i].astype(F32)
        spread = ((fcol == place) & (mod(lax.div(frow, jnp.int32(CAP)), FOLD) == q)).astype(F32).astype(BF16)
        total = total + dot(spread, summed.astype(BF16))
    total = total.astype(BF16)
    back[0] = total[:16]
    backs = [None]
    for dw in range(1, win):
        back_out[dw] = total[dw * 16 : (dw + 1) * 16]
        backs.append(send(back_out.at[dw], back.at[dw], back_s.at[dw], back_r.at[dw], other(-dw, 0)))
        backs[dw].start()

    for pair in logs:
        logs[pair].wait_recv()
    erow, ecol = iota((rows, win * 8), 0), iota((rows, win * 8), 1)
    edw = lax.div(erow, jnp.int32(16))
    expand = jnp.where(ecol == edw * 8 + mod(edw, 2) * CAP + mod(erow, CAP), 1.0, 0.0)
    den = jnp.zeros((rows, 1), F32)
    num = jnp.zeros((rows, 1), F32)
    for i in range(SPLIT):
        spread = jnp.dot(
            expand, logits[i].reshape(win * 8, lanes), preferred_element_type=F32, precision=lax.Precision.HIGHEST
        )
        score = jax.nn.sigmoid(spread)
        den = den + jnp.sum(jnp.where(mask[i] > 0.5, score, 0.0), axis=1, keepdims=True)
        num = num + jnp.sum(jnp.where(num_mask[i] > 0.5, score, 0.0), axis=1, keepdims=True)
    hot = onehot[...]
    filled = jnp.sum(hot, axis=1, keepdims=True) > 0.5
    weight = jnp.where(filled, 2.5 * num / jnp.where(filled, den, 1.0), 0.0)
    combine = (hot * weight).T
    high = combine.astype(BF16).astype(F32)
    middle = (combine - high).astype(BF16).astype(F32)
    low = combine - high - middle
    ccol = mod(lax.div(iota((rows_tok, rows), 1), jnp.int32(CAP)), FOLD)

    for dw in range(1, win):
        backs[dw].wait_recv()
    returned = back[...].reshape(rows, quarter)
    for q in range(FOLD):
        cols = slice(q * quarter, (q + 1) * quarter)
        acc = jnp.zeros((rows_tok, quarter), F32)
        for piece in (high, middle, low):
            acc = acc + dot(jnp.where(ccol == q, piece, 0.0).astype(BF16), returned)
        out[:, cols] = acc.astype(BF16)

    for copies in (disp[1:], rout.values(), backs[1:], fwd.values(), red.values(), logs.values()):
        for copy in copies:
            copy.wait_send()


def shards(tokens, expert_ids, lengths, router, w_gate, w_up, w_down):
    n = lax.axis_size("expert")
    win = n // SPLIT
    rows_tok, width = tokens.shape
    quarter = width // FOLD
    units = w_gate.shape[2]
    local = router.shape[0]
    epad = -(-local // 16) * 16
    if epad != local:
        router = jnp.pad(router, ((0, epad - local), (0, 0)))
    lanes = -(-win * epad // 128) * 128
    rows, per = win * 16, win * CAP
    vmem = pltpu.VMEM
    sems = pltpu.SemaphoreType.DMA
    scratch = [
        vmem((rows_tok, width), BF16),
        vmem(expert_ids.shape[::-1], jnp.int32),
        pltpu.SMEM(lengths.shape, jnp.int32),
        vmem((width, units), BF16),
        vmem((width, units), BF16),
        vmem((units, width), BF16),
        vmem((win, epad, width), BF16),
        vmem((win, 16, quarter), BF16),
        vmem((SPLIT, win, 16, quarter), BF16),
        vmem((SPLIT * per, width), BF16),
        vmem((SPLIT * per, units), BF16),
        vmem((FOLD, SPLIT, per, quarter), BF16),
        vmem((FOLD, SPLIT, per, quarter), BF16),
        vmem((win, 16, quarter), BF16),
        vmem((win, 16, quarter), BF16),
        vmem((SPLIT * per, lanes), F32),
        vmem((SPLIT, win, 8, lanes), F32),
        vmem((SPLIT, rows, lanes), F32),
        vmem((SPLIT, rows, lanes), F32),
        vmem((rows, rows_tok), F32),
        sems((7,)),
        *[sems((win,))] * 4,
        *[sems((win, SPLIT))] * 2,
        *[sems((FOLD, SPLIT))] * 2,
        *[sems((win,))] * 2,
        *[sems((SPLIT, win))] * 2,
    ]
    return pl.pallas_call(
        functools.partial(kernel, n, local),
        out_shape=jax.ShapeDtypeStruct((rows_tok, width), BF16),
        in_specs=[pl.BlockSpec(memory_space=pltpu.HBM)] * 7,
        out_specs=pl.BlockSpec(memory_space=pltpu.VMEM),
        scratch_shapes=scratch,
        compiler_params=pltpu.CompilerParams(
            collective_id=0, has_side_effects=True, vmem_limit_bytes=56 * 1024 * 1024
        ),
    )(tokens, expert_ids.T, lengths, router, w_gate, w_up, w_down)


def solution(mesh):
    placed = (
        P(("groups", "expert"), None),
        P(("groups", "expert"), None),
        P("groups"),
        P("expert", None),
        P("expert", None, None),
        P("expert", None, None),
        P("expert", None, None),
    )
    return jax.shard_map(
        shards, mesh=mesh, in_specs=placed, out_specs=P(("groups", "expert"), None), check_vma=False
    )
```

```python
import functools

import jax
import jax.numpy as jnp
from jax import lax
from jax.experimental import pallas as pl
from jax.experimental.pallas import tpu as pltpu
from jax.sharding import PartitionSpec as P

SPLIT = 4
SEQ_LEN = 2048
CAP = 4
FOLD = 16 // CAP
F32, BF16 = jnp.float32, jnp.bfloat16


def mod(a, b):
    return lax.rem(a, jnp.int32(b))


def iota(shape, axis):
    return lax.broadcasted_iota(jnp.int32, shape, axis)


def dot(a, b):
    return jnp.dot(a, b, preferred_element_type=F32)


def dot_nt(a, b):
    return lax.dot_general(a, b, (((1,), (1,)), ((), ())), preferred_element_type=F32)


def kernel(
    n, local, tokens_hbm, ids_hbm, len_hbm, router_hbm, gate_hbm, up_hbm, down_hbm, comb_out, back_hbm,
    tok, ids, length, wg, wu, wd, routed, fold_out, fold_in, x, hidden, part, reduced, back_out,
    logit, logits, mask, num_mask, onehot, back,
    load_sem, disp_s, disp_r, rout_s, rout_r, fwd_s, fwd_r, red_s, red_r, back_s, back_r, log_s, log_r,
):
    win = n // SPLIT
    rows = win * 16
    per = win * CAP
    rows_tok, width = tok.shape
    quarter = width // FOLD
    lanes = logit.shape[1]
    epad = routed.shape[1]
    me = lax.axis_index("expert")
    w = lax.div(me, jnp.int32(SPLIT))
    r = me - w * SPLIT

    def flip(at, bit):
        return at + bit - 2 * bit * mod(lax.div(at, jnp.int32(bit)), 2)

    def place_of(i):
        at = r
        for bit in (1, 2):
            at = flip(at, bit) if i & bit else at
        return at

    def other(dw, i):
        return {"expert": mod(w + (dw + win), win) * SPLIT + place_of(i)}

    loads = [
        pltpu.make_async_copy(src, dst, load_sem.at[i])
        for i, (src, dst) in enumerate(
            [
                (ids_hbm, ids), (len_hbm, length), (tokens_hbm, tok), (router_hbm, routed.at[0]),
                (gate_hbm.at[0], wg), (up_hbm.at[0], wu), (down_hbm.at[0], wd),
            ]
        )
    ]
    for load in loads:
        load.start()

    barrier = pltpu.get_barrier_semaphore()
    for step in range(1, n):
        pl.semaphore_signal(
            barrier, inc=1, device_id={"expert": mod(me + step, n)}, device_id_type=pl.DeviceIdType.MESH
        )

    def send(src, dst, s_sem, r_sem, device):
        copy = pltpu.make_async_remote_copy(
            src_ref=src, dst_ref=dst, send_sem=s_sem, recv_sem=r_sem,
            device_id=device, device_id_type=pl.DeviceIdType.MESH,
        )
        return copy

    loads[0].wait()
    loads[1].wait()
    ids_t = ids[...]
    ids_b = ids_t.astype(F32).astype(BF16)
    first = me * rows_tok
    alive = mod(first, SEQ_LEN) + iota((rows, rows_tok), 1) < length[lax.div(first, jnp.int32(SEQ_LEN))]
    row = iota((rows, rows_tok), 0)
    expert = mod(w + lax.div(row, jnp.int32(16)), win)
    chosen = ids_t[0:1, :] == expert
    for k in range(1, ids_t.shape[0]):
        chosen = chosen | (ids_t[k : k + 1, :] == expert)
    inside = jnp.where(chosen & alive, 1.0, 0.0)
    earlier = (iota((rows_tok, rows_tok), 0) < iota((rows_tok, rows_tok), 1)).astype(F32).astype(BF16)
    before = dot(inside.astype(BF16), earlier)
    hot = jnp.where(before == mod(row, CAP).astype(F32), inside, 0.0)
    onehot[...] = hot
    turn = mod(lax.div(row, jnp.int32(CAP)), FOLD)

    loads[2].wait()
    folded = jnp.zeros((rows, quarter), F32)
    for q in range(FOLD):
        picked = jnp.where(turn == q, hot, 0.0).astype(BF16)
        folded = folded + dot(picked, tok[:, q * quarter : (q + 1) * quarter])
    folded = folded.astype(BF16)
    fold_in[0, 0] = folded[:16]
    for dw in range(1, win):
        fold_out[dw] = folded[dw * 16 : (dw + 1) * 16]

    pl.semaphore_wait(barrier, n - 1)
    sends = []
    disp = [None]
    for dw in range(1, win):
        disp.append(send(fold_out.at[dw], fold_in.at[0, dw], disp_s.at[dw], disp_r.at[dw], other(dw, 0)))
        disp[dw].start()
    fwd = {}

    def forward(src, dst, dw, i):
        fwd[dw, dst] = send(
            fold_in.at[src, dw], fold_in.at[dst, dw], fwd_s.at[dw, dst], fwd_r.at[dw, dst], other(0, i)
        )
        fwd[dw, dst].start()

    for dw in range(win):
        if dw:
            disp[dw].wait_recv()
        forward(0, 2, dw, 2)
        forward(0, 1, dw, 1)

    loads[3].wait()
    rout, arrived = {}, set()

    def push(held):
        bit = (held & -held or win) // 2
        while bit:
            rout[held + bit] = send(
                routed.at[held], routed.at[held + bit], rout_s.at[held + bit], rout_r.at[held + bit],
                {"expert": flip(w, bit) * SPLIT + r},
            )
            rout[held + bit].start()
            bit //= 2

    def low_bit(d):
        return d & -d

    push(0)

    slot_ids = dot_nt(hot.astype(BF16), ids_b)
    srow = iota((rows, lanes), 0)
    lane = iota((rows, lanes), 1)
    slot_dw = lax.div(srow, jnp.int32(16))
    lane_dw = lax.div(lane, jnp.int32(epad))
    lane_e = lane - lane_dw * epad
    good = (lane_dw < win) & (lane_e < local)
    mine = mod(w + slot_dw, win)
    for i in range(SPLIT):
        chunk = (mine ^ lane_dw) * SPLIT + place_of(i)
        which = jnp.where(good, chunk * local + lane_e, -1)
        as_float = which.astype(F32)
        hit = jnp.zeros((rows, lanes), F32)
        for k in range(ids_b.shape[0]):
            hit = jnp.where(as_float == slot_ids[:, k : k + 1], 1.0, hit)
        mask[i] = hit
        num_mask[i] = jnp.where(which == mine, 1.0, 0.0)

    prow, pcol = iota((rows, rows), 0), iota((rows, rows), 1)
    q_of, dw_of, c_of = lax.div(prow, jnp.int32(per)), lax.div(mod(prow, per), jnp.int32(CAP)), mod(prow, CAP)
    perm = (pcol == dw_of * 16 + q_of * CAP + c_of).astype(F32).astype(BF16)
    for dw in range(win):
        fwd[dw, 2].wait_recv()
        forward(2, 3, dw, 1)
    for i in range(SPLIT):
        if i in (1, 3):
            for dw in range(win):
                fwd[dw, i].wait_recv()
        plain = dot(perm, fold_in[i].reshape(rows, quarter)).astype(BF16)
        for q in range(FOLD):
            x[i * per : (i + 1) * per, q * quarter : (q + 1) * quarter] = plain[q * per : (q + 1) * per]

    loads[4].wait()
    loads[5].wait()
    units = wg.shape[1]
    half = units // 2
    for piece in range(2):
        cols = slice(piece * half, (piece + 1) * half)
        g = dot(x[...], wg[:, cols])
        u = dot(x[...], wu[:, cols])
        hidden[:, cols] = (g * jax.nn.sigmoid(g) * u).astype(BF16)
    for held in sorted(range(1, win), key=lambda d: (-low_bit(d), d)):
        if low_bit(held) > 1:
            rout[held].wait_recv()
            arrived.add(held)
            push(held)
    loads[6].wait()
    red = {}

    def give(q, src, dst, i):
        red[q, dst] = send(part.at[q, src], reduced.at[q, dst], red_s.at[q, dst], red_r.at[q, dst], other(0, i))
        red[q, dst].start()

    for q in range(FOLD):
        part[q] = dot(hidden[...], wd[:, q * quarter : (q + 1) * quarter]).astype(BF16).reshape(
            SPLIT, per, quarter
        )
        give(q, 3, 3, 1)
        give(q, 1, 1, 1)
    for q in range(FOLD):
        red[q, 3].wait_recv()
        part[q, 2] = (part[q, 2].astype(F32) + reduced[q, 3].astype(F32)).astype(BF16)
        give(q, 2, 2, 2)

    for held in range(1, win):
        if held not in arrived:
            rout[held].wait_recv()
    logit[...] = jnp.zeros_like(logit)
    logit[:, : win * epad] = dot_nt(x[...], routed[...].reshape(win * epad, width))
    logs = {}
    for i in range(SPLIT):
        for dw in range(win):
            src = logit.at[pl.ds(i * per + dw // 2 * 8, 8)]
            if i or dw:
                logs[i, dw] = send(src, logits.at[i, dw], log_s.at[i, dw], log_r.at[i, dw], other(-dw, i))
                logs[i, dw].start()
            else:
                logits[0, 0] = logit[:8]

    frow, fcol = iota((rows, per), 0), iota((rows, per), 1)
    place = lax.div(frow, jnp.int32(16)) * CAP + mod(frow, CAP)
    total = jnp.zeros((rows, quarter), F32)
    for q in range(FOLD):
        summed = part[q, 0].astype(F32)
        for i in (1, 2):
            red[q, i].wait_recv()
            summed = summed + reduced[q, i].astype(F32)
        spread = ((fcol == place) & (mod(lax.div(frow, jnp.int32(CAP)), FOLD) == q)).astype(F32).astype(BF16)
        total = total + dot(spread, summed.astype(BF16))
    total = total.astype(BF16)
    back[0] = total[:16]
    backs = [None]
    for dw in range(1, win):
        back_out[dw] = total[dw * 16 : (dw + 1) * 16]
        backs.append(send(back_out.at[dw], back.at[dw], back_s.at[dw], back_r.at[dw], other(-dw, 0)))
        backs[dw].start()

    for pair in logs:
        logs[pair].wait_recv()
    erow, ecol = iota((rows, win * 8), 0), iota((rows, win * 8), 1)
    edw = lax.div(erow, jnp.int32(16))
    expand = jnp.where(ecol == edw * 8 + mod(edw, 2) * CAP + mod(erow, CAP), 1.0, 0.0)
    den = jnp.zeros((rows, 1), F32)
    num = jnp.zeros((rows, 1), F32)
    for i in range(SPLIT):
        spread = jnp.dot(
            expand, logits[i].reshape(win * 8, lanes), preferred_element_type=F32, precision=lax.Precision.HIGHEST
        )
        score = jax.nn.sigmoid(spread)
        den = den + jnp.sum(jnp.where(mask[i] > 0.5, score, 0.0), axis=1, keepdims=True)
        num = num + jnp.sum(jnp.where(num_mask[i] > 0.5, score, 0.0), axis=1, keepdims=True)
    hot = onehot[...]
    filled = jnp.sum(hot, axis=1, keepdims=True) > 0.5
    weight = jnp.where(filled, 2.5 * num / jnp.where(filled, den, 1.0), 0.0)
    combine = (hot * weight).T
    comb_out[...] = combine
    for dw in range(1, win):
        backs[dw].wait_recv()
    back_hbm[...] = back[...]

    for copies in (disp[1:], rout.values(), backs[1:], fwd.values(), red.values(), logs.values()):
        for copy in copies:
            copy.wait_send()


def mix(combine_ref, returned_ref, out_ref):
    combine = combine_ref[...]
    rows_tok, rows = combine.shape
    high = combine.astype(BF16).astype(F32)
    middle = (combine - high).astype(BF16).astype(F32)
    low = combine - high - middle
    returned = returned_ref[...].reshape(rows, returned_ref.shape[2])
    turn = mod(lax.div(iota((rows_tok, rows), 1), jnp.int32(CAP)), FOLD)
    acc = jnp.zeros(out_ref.shape, F32)
    for piece in (high, middle, low):
        acc = acc + dot(jnp.where(turn == pl.program_id(0), piece, 0.0).astype(BF16), returned)
    out_ref[...] = acc.astype(BF16)


def shards(tokens, expert_ids, lengths, router, w_gate, w_up, w_down):
    n = lax.axis_size("expert")
    win = n // SPLIT
    rows_tok, width = tokens.shape
    quarter = width // FOLD
    units = w_gate.shape[2]
    local = router.shape[0]
    epad = -(-local // 16) * 16
    if epad != local:
        router = jnp.pad(router, ((0, epad - local), (0, 0)))
    lanes = -(-win * epad // 128) * 128
    rows, per = win * 16, win * CAP
    vmem = pltpu.VMEM
    sems = pltpu.SemaphoreType.DMA
    scratch = [
        vmem((rows_tok, width), BF16),
        vmem(expert_ids.shape[::-1], jnp.int32),
        pltpu.SMEM(lengths.shape, jnp.int32),
        vmem((width, units), BF16),
        vmem((width, units), BF16),
        vmem((units, width), BF16),
        vmem((win, epad, width), BF16),
        vmem((win, 16, quarter), BF16),
        vmem((SPLIT, win, 16, quarter), BF16),
        vmem((SPLIT * per, width), BF16),
        vmem((SPLIT * per, units), BF16),
        vmem((FOLD, SPLIT, per, quarter), BF16),
        vmem((FOLD, SPLIT, per, quarter), BF16),
        vmem((win, 16, quarter), BF16),
        vmem((SPLIT * per, lanes), F32),
        vmem((SPLIT, win, 8, lanes), F32),
        vmem((SPLIT, rows, lanes), F32),
        vmem((SPLIT, rows, lanes), F32),
        vmem((rows, rows_tok), F32),
        vmem((win, 16, quarter), BF16),
        sems((7,)),
        *[sems((win,))] * 4,
        *[sems((win, SPLIT))] * 2,
        *[sems((FOLD, SPLIT))] * 2,
        *[sems((win,))] * 2,
        *[sems((SPLIT, win))] * 2,
    ]
    combine, returned = pl.pallas_call(
        functools.partial(kernel, n, local),
        out_shape=(
            jax.ShapeDtypeStruct((rows_tok, rows), F32),
            jax.ShapeDtypeStruct((win, 16, quarter), BF16),
        ),
        in_specs=[pl.BlockSpec(memory_space=pltpu.HBM)] * 7,
        out_specs=[pl.BlockSpec(memory_space=pltpu.VMEM)] * 2,
        scratch_shapes=scratch,
        compiler_params=pltpu.CompilerParams(
            collective_id=0, has_side_effects=True, vmem_limit_bytes=56 * 1024 * 1024
        ),
    )(tokens, expert_ids.T, lengths, router, w_gate, w_up, w_down)
    whole = pl.BlockSpec((rows_tok, rows), lambda q: (0, 0))
    return pl.pallas_call(
        mix,
        grid=(FOLD,),
        out_shape=jax.ShapeDtypeStruct((rows_tok, width), BF16),
        in_specs=[whole, pl.BlockSpec((win, 16, quarter), lambda q: (0, 0, 0))],
        out_specs=pl.BlockSpec((rows_tok, quarter), lambda q: (0, q)),
    )(combine, returned)


def solution(mesh):
    placed = (
        P(("groups", "expert"), None),
        P(("groups", "expert"), None),
        P("groups"),
        P("expert", None),
        P("expert", None, None),
        P("expert", None, None),
        P("expert", None, None),
    )
    return jax.shard_map(
        shards, mesh=mesh, in_specs=placed, out_specs=P(("groups", "expert"), None), check_vma=False
    )
```
